32 devices in a mesh: group: 2 (over y), out: 4 (over z), in: 2 (over x), tok: 2 (over core).
Axes of the slice: x: 2, y: 2, z: 4, core: 2. Of those that a mesh axis runs over, the one named last changes fastest.
Arguments:
- inputs: bfloat16 [864, 6144], P(('group', 'tok'), 'in'), parts along dimension 0, may hold values from -6 to 6
- grad_act: bfloat16 [864, 24576], P(('group', 'tok'), 'out'), parts along dimension 0, may hold values from -6 to 6
- weight: bfloat16 [6144, 24576], P(('in', 'tok'), 'out'), may hold values from -0.078125 to 0.078125
- score: bfloat16 [6144, 24576], P(('in', 'tok'), 'out'), may hold values from -1.1953125 to 1.1953125
Outputs:
- grad_inputs: bfloat16 [864, 6144], P(('group', 'tok'), 'in'), parts along dimension 0
- new_score: bfloat16 [12288, 24576], P(('group', 'in', 'tok'), 'out'), parts along dimension 0
The draws below stay inside these ranges and needn't reach their ends.
There are 2 independent parts, one for each index of `group`. The reference program is written for one: setup_inputs(seed, part) draws one part's arguments, and reference() takes and returns one part's arrays. A program takes and returns all parts, laid end to end along the dimension named above; an argument that names none is the same for every part. Nothing has to cross between parts.
All inputs are finite; a program needn't handle non-finite values.
Results may differ from the reference program's by a relative error of at most 0.005.
Values may be sent and summed in bfloat16 or wider, within the bound.
A program may use at most 256 MiB of HBM per device.

```python
import jax
import jax.numpy as jnp
from jax import lax

D = 6144
FF = 24576
TOKENS = 432
N_OUT = 4


def shard_levels(stream_key, extent, shards, low, high):
    level = 1.0
    for dim, blocks in shards:
        draws = jax.random.uniform(jax.random.fold_in(jax.random.fold_in(stream_key, 6), dim), (blocks,), jnp.float32, low / len(shards), high / len(shards))
        level = level * jnp.repeat(jnp.exp(draws), extent[dim] // blocks).reshape((-1,) + (1,) * (len(extent) - 1 - dim))
    return level


def scatter_about(rng, extent, scale, limit, split=(), held_as=jnp.bfloat16):
    loudness = shard_levels(rng, extent, split, -0.22, 0.18) if split else 1.0
    entries = jax.random.normal(rng, extent, jnp.float32) * scale * loudness
    return jnp.minimum(jnp.maximum(entries, -limit), limit).astype(held_as)


def setup_inputs(seed: int = 0, part: int = 0) -> dict:
    keys = jax.random.split(jax.random.key(seed), 5)
    part_splits = jax.random.split(jax.random.fold_in(keys[4], part), 5)
    return {
        "inputs": scatter_about(part_splits[0], (TOKENS, D), 1.0, 6.0, ((0, 2), (1, 2))),
        "grad_act": scatter_about(part_splits[1], (TOKENS, FF), 1.0, 6.0, ((0, 2), (1, 4))),
        "weight": scatter_about(keys[2], (D, FF), D ** -0.5, 0.078125, ((0, 4), (1, 4))),
        "score": scatter_about(keys[3], (D, FF), 0.2, 1.1953125, ((0, 4), (1, 4))),
    }


def gelu_slope(pre):
    cdf = 0.5 * (1.0 + jax.scipy.special.erf(pre * 0.7071067811865476))
    return cdf + pre * jnp.exp(-0.5 * pre * pre) * 0.3989422804014327


def reference(inputs, grad_act, weight, score):
    width = FF // N_OUT
    count = FF // width

    def step(carry, index):
        start = (index * width).astype(jnp.int32)
        w_block = lax.dynamic_slice_in_dim(weight, start, width, 1)
        s_block = lax.dynamic_slice_in_dim(score, start, width, 1)
        g_block = lax.dynamic_slice_in_dim(grad_act, start, width, 1)
        pre = jnp.dot(inputs, w_block, preferred_element_type=jnp.float32)
        grad_pre = (g_block.astype(jnp.float32) * gelu_slope(pre)).astype(jnp.bfloat16)
        grad_w = jnp.dot(inputs.T, grad_pre, preferred_element_type=jnp.float32)
        fresh = (s_block.astype(jnp.float32) - w_block.astype(jnp.float32) * grad_w).astype(jnp.bfloat16)
        carry = carry + jnp.dot(grad_pre, w_block.T, preferred_element_type=jnp.float32)
        return carry, fresh

    start_sum = jnp.zeros((inputs.shape[0], inputs.shape[1]), jnp.float32)
    total, blocks = lax.scan(step, start_sum, jnp.arange(count, dtype=jnp.int32))
    new_score = jnp.transpose(blocks, (1, 0, 2)).reshape(weight.shape[0], FF)
    return total.astype(jnp.bfloat16), new_score
```

```python
import jax
import jax.numpy as jnp
from jax import lax
from jax.sharding import PartitionSpec as P

BF = jnp.bfloat16
F32 = jnp.float32


def gelu_slope(pre):
    cdf = 0.5 * (1.0 + jax.scipy.special.erf(pre * 0.7071067811865476))
    return cdf + pre * jnp.exp(-0.5 * pre * pre) * 0.3989422804014327


def swap(x):
    return lax.ppermute(x, "tok", [(0, 1), (1, 0)])


def mm(a, b, dims):
    return lax.dot_general(a, b, (dims, ((), ())), preferred_element_type=F32)


def sum_over(x, axis, n):
    if n == 1:
        return x
    if n == 2:
        return x + lax.ppermute(x.astype(BF), axis, [(0, 1), (1, 0)]).astype(F32)
    return lax.psum(x, axis)


def reduce_out(x, axis, n):
    if n == 1:
        return x.astype(BF)
    if n > 8 or x.shape[1] % (128 * n):
        return lax.psum(x, axis).astype(BF)
    w = x.shape[1] // n
    me = lax.axis_index(axis)
    total = lax.dynamic_slice_in_dim(x, me * w, w, 1)
    xb = x.astype(BF)
    for k in range(1, n):
        to = lax.rem(me + k, n)
        piece = lax.dynamic_slice_in_dim(xb, to * w, w, 1)
        got = lax.ppermute(piece, axis, [(i, (i + k) % n) for i in range(n)])
        total = total + got.astype(F32)
    mine = total.astype(BF)
    out = jnp.zeros(x.shape, BF)
    out = lax.dynamic_update_slice_in_dim(out, mine, me * w, 1)
    for k in range(1, n):
        got = lax.ppermute(mine, axis, [(i, (i + k) % n) for i in range(n)])
        out = lax.dynamic_update_slice_in_dim(out, got, lax.rem(me - k + n, n) * w, 1)
    return out


def make(n_in, n_out):
    def on_device(inputs, grad_act, weight, score):
        rows, ff = weight.shape
        t = lax.axis_index("tok")
        x_mine = lax.dynamic_slice_in_dim(inputs, t * rows, rows, 1)
        x_other = swap(lax.dynamic_slice_in_dim(inputs, (1 - t) * rows, rows, 1))
        chunks = 4 if ff % (4 * 256) == 0 else 1
        w = ff // chunks
        gm, go = [], []
        for c in range(chunks):
            wc = weight[:, c * w : (c + 1) * w]
            send = mm(x_other, wc, ((1,), (0,))).astype(BF)
            part = mm(x_mine, wc, ((1,), (0,))) + swap(send).astype(F32)
            pre = sum_over(part, "in", n_in)
            g = (grad_act[:, c * w : (c + 1) * w].astype(F32) * gelu_slope(pre)).astype(BF)
            gm.append(g)
            go.append(swap(g))
        gm = jnp.concatenate(gm, axis=1)
        go = jnp.concatenate(go, axis=1)
        dx_other = mm(go, weight, ((1,), (1,))).astype(BF)
        dx_mine = mm(gm, weight, ((1,), (1,)))
        dx_got = swap(dx_other).astype(F32)
        lo = jnp.where(t == 0, dx_mine, dx_got)
        hi = jnp.where(t == 0, dx_got, dx_mine)
        grad_inputs = reduce_out(jnp.concatenate([lo, hi], axis=1), "out", n_out)
        xs = jnp.concatenate([x_mine, x_other], axis=0)
        gs = jnp.concatenate([gm, go], axis=0)
        grad_w = mm(xs, gs, ((0,), (0,)))
        new_score = (score.astype(F32) - weight.astype(F32) * grad_w).astype(BF)
        return grad_inputs, new_score

    return on_device


def solution(mesh):
    placed = (
        P(("group", "tok"), "in"),
        P(("group", "tok"), "out"),
        P(("in", "tok"), "out"),
        P(("in", "tok"), "out"),
    )
    return jax.shard_map(
        make(mesh.shape["in"], mesh.shape["out"]),
        mesh=mesh,
        in_specs=placed,
        out_specs=(P(("group", "tok"), "in"), P(("group", "in", "tok"), "out")),
        check_vma=False,
    )
```

```python
import jax
import jax.numpy as jnp
from jax import lax
from jax.experimental import pallas as pl
from jax.experimental.pallas import tpu as pltpu
from jax.sharding import PartitionSpec as P

BF = jnp.bfloat16
F32 = jnp.float32


def gelu_slope(pre):
    cdf = 0.5 * (1.0 + jax.scipy.special.erf(pre * 0.7071067811865476))
    return cdf + pre * jnp.exp(-0.5 * pre * pre) * 0.3989422804014327


def swap(x):
    return lax.ppermute(x, "tok", [(0, 1), (1, 0)])


def mm(a, b, dims):
    return lax.dot_general(a, b, (dims, ((), ())), preferred_element_type=F32)


def sum_over(x, axis, n):
    if n == 1:
        return x
    if n == 2:
        return x + lax.ppermute(x.astype(BF), axis, [(0, 1), (1, 0)]).astype(F32)
    return lax.psum(x, axis)


def reduce_out(x, axis, n):
    if n == 1:
        return x.astype(BF)
    if n > 8 or x.shape[1] % (128 * n):
        return lax.psum(x, axis).astype(BF)
    w = x.shape[1] // n
    me = lax.axis_index(axis)
    total = lax.dynamic_slice_in_dim(x, me * w, w, 1)
    xb = x.astype(BF)
    for k in range(1, n):
        to = lax.rem(me + k, n)
        piece = lax.dynamic_slice_in_dim(xb, to * w, w, 1)
        got = lax.ppermute(piece, axis, [(i, (i + k) % n) for i in range(n)])
        total = total + got.astype(F32)
    mine = total.astype(BF)
    out = jnp.zeros(x.shape, BF)
    out = lax.dynamic_update_slice_in_dim(out, mine, me * w, 1)
    for k in range(1, n):
        got = lax.ppermute(mine, axis, [(i, (i + k) % n) for i in range(n)])
        out = lax.dynamic_update_slice_in_dim(out, got, lax.rem(me - k + n, n) * w, 1)
    return out


def block_of(n, sizes):
    for b in sizes:
        if n % b == 0:
            return b
    return n


def dx_kernel(g_ref, w_ref, o_ref):
    @pl.when(pl.program_id(0) == 0)
    def _():
        o_ref[...] = jnp.zeros_like(o_ref)

    o_ref[...] += lax.dot_general(
        g_ref[...], w_ref[...], (((1,), (1,)), ((), ())), preferred_element_type=F32
    )


def dx_partial(g, weight):
    rows, ff = weight.shape
    m = g.shape[0]
    w = block_of(ff, (768, 512, 256, 128))
    return pl.pallas_call(
        dx_kernel,
        grid=(ff // w,),
        in_specs=[
            pl.BlockSpec((m, w), lambda i: (0, i)),
            pl.BlockSpec((rows, w), lambda i: (0, i)),
        ],
        out_specs=pl.BlockSpec((m, rows), lambda i: (0, 0)),
        out_shape=jax.ShapeDtypeStruct((m, rows), F32),
        cost_estimate=pl.CostEstimate(
            flops=2 * m * rows * ff, bytes_accessed=2 * rows * ff, transcendentals=0
        ),
        compiler_params=pltpu.CompilerParams(vmem_limit_bytes=32 * 2**20),
    )(g, weight)


def score_kernel(x_ref, g_ref, w_ref, s_ref, *rest):
    o_ref = rest[-1]
    rows = w_ref.shape[0]
    step = block_of(rows, (384, 256, 128))
    for r in range(0, rows, step):
        part = pl.ds(r, step)
        gw = jnp.dot(x_ref[part, :], g_ref[...], preferred_element_type=F32)
        o_ref[part, :] = (
            s_ref[part, :].astype(F32) - w_ref[part, :].astype(F32) * gw
        ).astype(BF)


def score_part(x_t, g, weight, score, first, count, w, earlier):
    rows, ff = weight.shape
    m = g.shape[0]
    block = pl.BlockSpec((rows, w), lambda i: (0, i + first))
    specs = [
        pl.BlockSpec((rows, m), lambda i: (0, 0)),
        pl.BlockSpec((m, w), lambda i: (0, i + first)),
        block,
        block,
    ]
    args = [x_t, g, weight, score]
    alias = {}
    if earlier is not None:
        specs.append(pl.BlockSpec(memory_space=pl.ANY))
        args.append(earlier)
        alias = {4: 0}
    return pl.pallas_call(
        score_kernel,
        grid=(count,),
        in_specs=specs,
        out_specs=block,
        out_shape=jax.ShapeDtypeStruct((rows, ff), BF),
        input_output_aliases=alias,
        cost_estimate=pl.CostEstimate(
            flops=2 * m * rows * w * count,
            bytes_accessed=6 * rows * w * count,
            transcendentals=0,
        ),
        compiler_params=pltpu.CompilerParams(vmem_limit_bytes=40 * 2**20),
    )(*args)


def make(n_in, n_out):
    def on_device(inputs, grad_act, weight, score):
        rows, ff = weight.shape
        tokens = inputs.shape[0]
        t = lax.axis_index("tok")
        x_mine = lax.dynamic_slice_in_dim(inputs, t * rows, rows, 1)
        x_other = swap(lax.dynamic_slice_in_dim(inputs, (1 - t) * rows, rows, 1))
        chunks = 2 if ff % 512 == 0 else 1
        w = ff // chunks
        cut = -(-tokens // 32) * 16
        spans = [(0, cut), (cut, tokens)]
        parts = []
        token = None
        for lo, hi in spans:
            xs = jnp.concatenate([x_mine[lo:hi], x_other[lo:hi]], axis=0)
            sends = []
            for c in range(chunks):
                if token is not None:
                    xs, token = lax.optimization_barrier((xs, token))
                both = mm(xs, weight[:, c * w : (c + 1) * w], ((1,), (0,)))
                token = both[hi - lo :].astype(BF)
                sends.append(both[: hi - lo] + swap(token).astype(F32))
            parts.append(sends)
        gs, terms = [], []
        for (lo, hi), sends in zip(spans, parts):
            gm, go = [], []
            for c in range(chunks):
                pre = sum_over(sends[c], "in", n_in)
                act = grad_act[lo:hi, c * w : (c + 1) * w]
                g = (act.astype(F32) * gelu_slope(pre)).astype(BF)
                gm.append(g)
                go.append(swap(g))
            g = jnp.concatenate(
                [jnp.concatenate(gm, axis=1), jnp.concatenate(go, axis=1)], axis=0
            )
            gs.append(g)
            dx = dx_partial(g, weight)
            mine, got = dx[: hi - lo], swap(dx[hi - lo :].astype(BF)).astype(F32)
            left = jnp.where(t == 0, mine, got)
            right = jnp.where(t == 0, got, mine)
            terms.append(jnp.concatenate([left, right], axis=1))
        grad_inputs = jnp.concatenate(
            [reduce_out(term, "out", n_out) for term in terms], axis=0
        )
        x_t = jnp.concatenate(
            [x[lo:hi] for lo, hi in spans for x in (x_mine, x_other)], axis=0
        ).T
        g = jnp.concatenate(gs, axis=0)
        wb = block_of(ff, (512, 256, 128))
        half = ff // wb // 2
        new_score = None
        for first, count in ((0, half), (half, ff // wb - half)):
            if count:
                new_score = score_part(
                    x_t, g, weight, score, first, count, wb, new_score
                )
        return grad_inputs, new_score

    return on_device


def solution(mesh):
    placed = (
        P(("group", "tok"), "in"),
        P(("group", "tok"), "out"),
        P(("in", "tok"), "out"),
        P(("in", "tok"), "out"),
    )
    return jax.shard_map(
        make(mesh.shape["in"], mesh.shape["out"]),
        mesh=mesh,
        in_specs=placed,
        out_specs=(P(("group", "tok"), "in"), P(("group", "in", "tok"), "out")),
        check_vma=False,
    )
```

```python
import functools

import jax
import jax.numpy as jnp
from jax import lax
from jax.experimental import pallas as pl
from jax.experimental.pallas import tpu as pltpu
from jax.sharding import PartitionSpec as P

BF = jnp.bfloat16
F32 = jnp.float32


def gelu_slope(pre):
    cdf = 0.5 * (1.0 + jax.scipy.special.erf(pre * 0.7071067811865476))
    return cdf + pre * jnp.exp(-0.5 * pre * pre) * 0.3989422804014327


def swap(x):
    return lax.ppermute(x, "tok", [(0, 1), (1, 0)])


def mm(a, b, dims):
    return lax.dot_general(a, b, (dims, ((), ())), preferred_element_type=F32)


def after(x, *others):
    return lax.optimization_barrier((x,) + others)[0]


def send_partial(part, n):
    if n == 2:
        return part, lax.ppermute(part.astype(BF), "in", [(0, 1), (1, 0)])
    return None, lax.psum(part, "in")


def direct(x, n):
    return 1 < n <= 8 and x.shape[1] % (128 * n) == 0


def scatter_out(x, n):
    w = x.shape[1] // n
    me = lax.axis_index("out")
    total = lax.dynamic_slice_in_dim(x, me * w, w, 1)
    xb = x.astype(BF)
    for k in range(1, n):
        to = lax.rem(me + k, n)
        piece = lax.dynamic_slice_in_dim(xb, to * w, w, 1)
        got = lax.ppermute(piece, "out", [(i, (i + k) % n) for i in range(n)])
        total = total + got.astype(F32)
    return total.astype(BF), xb


def gather_out(mine, n):
    w = mine.shape[1]
    me = lax.axis_index("out")
    out = jnp.zeros((mine.shape[0], w * n), BF)
    out = lax.dynamic_update_slice_in_dim(out, mine, me * w, 1)
    for k in range(1, n):
        got = lax.ppermute(mine, "out", [(i, (i + k) % n) for i in range(n)])
        out = lax.dynamic_update_slice_in_dim(out, got, lax.rem(me - k + n, n) * w, 1)
    return out


def block_of(n, sizes):
    for b in sizes:
        if n % b == 0:
            return b
    return n


def dx_kernel(m_ref, o_ref, w_ref, init_ref, sum_ref):
    @pl.when(pl.program_id(0) == 0)
    def _():
        sum_ref[...] = init_ref[...]

    g = jnp.concatenate([m_ref[...], o_ref[...]], axis=0)
    sum_ref[...] += lax.dot_general(
        g, w_ref[...], (((1,), (1,)), ((), ())), preferred_element_type=F32
    )


def dx_partial(mine, other, weight, start, unit, init):
    rows = weight.shape[0]
    m, width = mine.shape
    first = start // unit
    g_block = pl.BlockSpec((m, unit), lambda i: (0, i))
    whole = pl.BlockSpec((2 * m, rows), lambda i: (0, 0))
    return pl.pallas_call(
        dx_kernel,
        grid=(width // unit,),
        in_specs=[
            g_block,
            g_block,
            pl.BlockSpec((rows, unit), lambda i: (0, i + first)),
            whole,
        ],
        out_specs=whole,
        out_shape=jax.ShapeDtypeStruct((2 * m, rows), F32),
        cost_estimate=pl.CostEstimate(
            flops=4 * m * rows * width, bytes_accessed=2 * rows * width, transcendentals=0
        ),
        compiler_params=pltpu.CompilerParams(vmem_limit_bytes=32 * 2**20),
    )(mine, other, weight, init)


def score_kernel(parts, x_ref, *refs):
    g_refs, (w_ref, s_ref), o_ref = refs[:parts], refs[parts : parts + 2], refs[-1]
    rows = w_ref.shape[0]
    step = block_of(rows, (384, 256, 128))
    g = jnp.concatenate([ref[...] for ref in g_refs], axis=0)
    for r in range(0, rows, step):
        part = pl.ds(r, step)
        gw = jnp.dot(x_ref[part, :], g, preferred_element_type=F32)
        o_ref[part, :] = (
            s_ref[part, :].astype(F32) - w_ref[part, :].astype(F32) * gw
        ).astype(BF)


def score_part(x_t, gs, weight, score, start, w, earlier):
    rows, ff = weight.shape
    m, width = gs[0].shape
    first, count = start // w, width // w
    block = pl.BlockSpec((rows, w), lambda i: (0, i + first))
    specs = [pl.BlockSpec(x_t.shape, lambda i: (0, 0))]
    specs += [pl.BlockSpec((m, w), lambda i: (0, i)) for _ in gs]
    specs += [block, block]
    args = [x_t, *gs, weight, score]
    alias = {}
    if earlier is not None:
        alias = {len(args): 0}
        specs.append(pl.BlockSpec(memory_space=pl.ANY))
        args.append(earlier)
    return pl.pallas_call(
        functools.partial(score_kernel, len(gs)),
        grid=(count,),
        in_specs=specs,
        out_specs=block,
        out_shape=jax.ShapeDtypeStruct((rows, ff), BF),
        input_output_aliases=alias,
        cost_estimate=pl.CostEstimate(
            flops=2 * x_t.shape[1] * rows * width,
            bytes_accessed=6 * rows * width,
            transcendentals=0,
        ),
        compiler_params=pltpu.CompilerParams(vmem_limit_bytes=40 * 2**20),
    )(*args)


def make(n_in, n_out):
    def on_device(inputs, grad_act, weight, score):
        rows, ff = weight.shape
        tokens = inputs.shape[0]
        t = lax.axis_index("tok")
        cut = -(-tokens // 32) * 16
        pad = ((0, 2 * cut - tokens), (0, 0))
        spans = [(0, cut), (cut, tokens)]
        x_other = swap(lax.dynamic_slice_in_dim(inputs, (1 - t) * rows, rows, 1))
        x_mine = lax.dynamic_slice_in_dim(inputs, t * rows, rows, 1)
        unit = block_of(ff, (512, 256, 128))
        small = max(1, ff // unit // 4) * unit
        chunks = [(0, small), (small, ff)] if small < ff else [(0, ff)]
        sent = {}
        token = None
        for h, (lo, hi) in enumerate(spans):
            for a, b in chunks if h == 0 else chunks[::-1]:
                theirs, own = x_other[lo:hi], x_mine[lo:hi]
                if token is not None:
                    theirs = after(theirs, token)
                wc = weight[:, a:b]
                token = mm(theirs, wc, ((1,), (0,))).astype(BF)
                part = mm(own, wc, ((1,), (0,))) + swap(token).astype(F32)
                if not sent:
                    token = part
                sent[h, a] = send_partial(part, n_in)
        g_of, outs = {}, []
        waits = [[], []]
        for h, (lo, hi) in enumerate(spans):
            total = jnp.zeros((2 * cut, rows), F32)
            order = chunks if h == 0 else chunks[::-1]
            for i, (a, b) in enumerate(order):
                own, got = sent[h, a]
                if h == 1:
                    got = after(got, *waits[0 if i == 0 else 1])
                pre = got.astype(F32) if own is None else own + got.astype(F32)
                g = (grad_act[lo:hi, a:b].astype(F32) * gelu_slope(pre)).astype(BF)
                if hi - lo < cut:
                    g = jnp.pad(g, pad)
                g_of[h, a] = (g, swap(g))
                total = dx_partial(*g_of[h, a], weight, a, unit, total)
            mine, theirs = total[: hi - lo], total[cut : cut + hi - lo]
            got = swap(theirs.astype(BF)).astype(F32)
            left, right = jnp.where(t == 0, mine, got), jnp.where(t == 0, got, mine)
            term = jnp.concatenate([left, right], axis=1)
            if direct(term, n_out):
                piece, ready = scatter_out(term, n_out)
                waits = [[ready], [piece]]
                outs.append(gather_out(piece, n_out))
            else:
                waits = [[term], [term]]
                outs.append(lax.psum(term, "out").astype(BF))
        xs = []
        for lo, hi in spans:
            for x in (x_mine, x_other):
                xs.append(x[lo:hi] if hi - lo == cut else jnp.pad(x[lo:hi], pad))
        x_t = jnp.concatenate(xs, axis=0).T
        new_score = None
        for i, (a, b) in enumerate(chunks[::-1]):
            x_now = after(x_t, *waits[0 if i == 0 else 1])
            gs = [*g_of[0, a], *g_of[1, a]]
            new_score = score_part(x_now, gs, weight, score, a, unit, new_score)
        return jnp.concatenate(outs, axis=0), new_score

    return on_device


def solution(mesh):
    placed = (
        P(("group", "tok"), "in"),
        P(("group", "tok"), "out"),
        P(("in", "tok"), "out"),
        P(("in", "tok"), "out"),
    )
    return jax.shard_map(
        make(mesh.shape["in"], mesh.shape["out"]),
        mesh=mesh,
        in_specs=placed,
        out_specs=(P(("group", "tok"), "in"), P(("group", "in", "tok"), "out")),
        check_vma=False,
    )
```

```python
import functools

import jax
import jax.numpy as jnp
from jax import lax
from jax.experimental import pallas as pl
from jax.experimental.pallas import tpu as pltpu
from jax.sharding import PartitionSpec as P

BF = jnp.bfloat16
F32 = jnp.float32


def gelu_slope(pre):
    cdf = 0.5 * (1.0 + jax.scipy.special.erf(pre * 0.7071067811865476))
    return cdf + pre * jnp.exp(-0.5 * pre * pre) * 0.3989422804014327


def swap(x):
    return lax.ppermute(x, "tok", [(0, 1), (1, 0)])


def mm(a, b, dims):
    return lax.dot_general(a, b, (dims, ((), ())), preferred_element_type=F32)


def after(x, *others):
    return lax.optimization_barrier((x,) + others)[0]


def send_partial(part, n):
    if n == 2:
        return part, lax.ppermute(part.astype(BF), "in", [(0, 1), (1, 0)])
    return None, lax.psum(part, "in")


def direct(x, n):
    return 1 < n <= 8 and x.shape[1] % (128 * n) == 0


def scatter_out(x, n):
    w = x.shape[1] // n
    me = lax.axis_index("out")
    total = lax.dynamic_slice_in_dim(x, me * w, w, 1)
    xb = x.astype(BF)
    for k in range(1, n):
        to = lax.rem(me + k, n)
        piece = lax.dynamic_slice_in_dim(xb, to * w, w, 1)
        got = lax.ppermute(piece, "out", [(i, (i + k) % n) for i in range(n)])
        total = total + got.astype(F32)
    return total.astype(BF), xb


def gather_out(mine, n):
    w = mine.shape[1]
    me = lax.axis_index("out")
    out = jnp.zeros((mine.shape[0], w * n), BF)
    out = lax.dynamic_update_slice_in_dim(out, mine, me * w, 1)
    for k in range(1, n):
        got = lax.ppermute(mine, "out", [(i, (i + k) % n) for i in range(n)])
        out = lax.dynamic_update_slice_in_dim(out, got, lax.rem(me - k + n, n) * w, 1)
    return out


def block_of(n, sizes):
    for b in sizes:
        if n % b == 0:
            return b
    return n


def dx_kernel(m_ref, o_ref, w_ref, sum_ref, acc_ref):
    i = pl.program_id(0)

    @pl.when(i == 0)
    def _():
        acc_ref[...] = jnp.zeros_like(acc_ref)

    g = jnp.concatenate([m_ref[...], o_ref[...]], axis=0)
    acc_ref[...] += lax.dot_general(
        w_ref[...], g, (((1,), (1,)), ((), ())), preferred_element_type=F32
    )

    @pl.when(i == pl.num_programs(0) - 1)
    def _():
        sum_ref[...] = acc_ref[...].T


def dx_partial(mine, other, weight, unit):
    rows = weight.shape[0]
    m, width = mine.shape
    g_block = pl.BlockSpec((m, unit), lambda i: (0, i))
    whole = pl.BlockSpec((2 * m, rows), lambda i: (0, 0))
    return pl.pallas_call(
        dx_kernel,
        grid=(width // unit,),
        in_specs=[
            g_block,
            g_block,
            pl.BlockSpec((rows, unit), lambda i: (0, i)),
        ],
        out_specs=whole,
        out_shape=jax.ShapeDtypeStruct((2 * m, rows), F32),
        scratch_shapes=[pltpu.VMEM((rows, 2 * m), F32)],
        cost_estimate=pl.CostEstimate(
            flops=4 * m * rows * width, bytes_accessed=2 * rows * width, transcendentals=0
        ),
        compiler_params=pltpu.CompilerParams(vmem_limit_bytes=48 * 2**20),
    )(mine, other, weight)


def score_kernel(parts, x_ref, *refs):
    g_refs, (w_ref, s_ref), o_ref = refs[:parts], refs[parts : parts + 2], refs[-1]
    rows = w_ref.shape[0]
    step = block_of(rows, (384, 256, 128))
    g = jnp.concatenate([ref[...] for ref in g_refs], axis=0)
    for r in range(0, rows, step):
        part = pl.ds(r, step)
        gw = jnp.dot(x_ref[part, :], g, preferred_element_type=F32)
        o_ref[part, :] = (
            s_ref[part, :].astype(F32) - w_ref[part, :].astype(F32) * gw
        ).astype(BF)


def score_part(x_t, gs, weight, score, first, count, w, earlier):
    rows, ff = weight.shape
    m, width = gs[0].shape[0], count * w
    block = pl.BlockSpec((rows, w), lambda i: (0, i + first))
    specs = [pl.BlockSpec(x_t.shape, lambda i: (0, 0))]
    specs += [pl.BlockSpec((m, w), lambda i: (0, i + first)) for _ in gs]
    specs += [block, block]
    args = [x_t, *gs, weight, score]
    alias = {}
    if earlier is not None:
        alias = {len(args): 0}
        specs.append(pl.BlockSpec(memory_space=pl.ANY))
        args.append(earlier)
    return pl.pallas_call(
        functools.partial(score_kernel, len(gs)),
        grid=(count,),
        in_specs=specs,
        out_specs=block,
        out_shape=jax.ShapeDtypeStruct((rows, ff), BF),
        input_output_aliases=alias,
        cost_estimate=pl.CostEstimate(
            flops=2 * x_t.shape[1] * rows * width,
            bytes_accessed=6 * rows * width,
            transcendentals=0,
        ),
        compiler_params=pltpu.CompilerParams(vmem_limit_bytes=40 * 2**20),
    )(*args)


def make(n_in, n_out):
    def on_device(inputs, grad_act, weight, score):
        rows, ff = weight.shape
        tokens = inputs.shape[0]
        t = lax.axis_index("tok")
        full = -(-tokens // 16) * 16
        pad = ((0, full - tokens), (0, 0))
        x_mine = lax.dynamic_slice_in_dim(inputs, t * rows, rows, 1)
        x_other = swap(lax.dynamic_slice_in_dim(inputs, (1 - t) * rows, rows, 1))
        chunks = 4 if ff % (4 * 256) == 0 else 1
        w = ff // chunks
        gm, go = [], []
        for c in range(chunks):
            wc = weight[:, c * w : (c + 1) * w]
            send = mm(x_other, wc, ((1,), (0,))).astype(BF)
            part = mm(x_mine, wc, ((1,), (0,))) + swap(send).astype(F32)
            own, got = send_partial(part, n_in)
            pre = got if own is None else own + got.astype(F32)
            g = (grad_act[:, c * w : (c + 1) * w].astype(F32) * gelu_slope(pre)).astype(BF)
            g = jnp.pad(g, pad)
            gm.append(g)
            go.append(swap(g))
        gs = [jnp.concatenate(gm, axis=1), jnp.concatenate(go, axis=1)]
        unit = block_of(ff, (512, 256, 128))
        total = dx_partial(*gs, weight, unit)
        mine, theirs = total[:tokens], total[full : full + tokens]
        got = swap(theirs.astype(BF)).astype(F32)
        left, right = jnp.where(t == 0, mine, got), jnp.where(t == 0, got, mine)
        term = jnp.concatenate([left, right], axis=1)
        if direct(term, n_out):
            piece, ready = scatter_out(term, n_out)
            waits = [ready, piece]
            grad_inputs = gather_out(piece, n_out)
        else:
            waits = [term, term]
            grad_inputs = lax.psum(term, "out").astype(BF)
        x_t = jnp.concatenate([jnp.pad(x_mine, pad), jnp.pad(x_other, pad)], axis=0).T
        blocks = ff // unit
        half = (blocks + 1) // 2
        new_score = None
        for wait, first, count in ((waits[0], 0, half), (waits[1], half, blocks - half)):
            if count:
                x_now = after(x_t, wait)
                new_score = score_part(
                    x_now, gs, weight, score, first, count, unit, new_score
                )
        return grad_inputs, new_score

    return on_device


def solution(mesh):
    placed = (
        P(("group", "tok"), "in"),
        P(("group", "tok"), "out"),
        P(("in", "tok"), "out"),
        P(("in", "tok"), "out"),
    )
    return jax.shard_map(
        make(mesh.shape["in"], mesh.shape["out"]),
        mesh=mesh,
        in_specs=placed,
        out_specs=(P(("group", "tok"), "in"), P(("group", "in", "tok"), "out")),
        check_vma=False,
    )
```

```python
import functools

import jax
import jax.numpy as jnp
from jax import lax
from jax.experimental import pallas as pl
from jax.experimental.pallas import tpu as pltpu
from jax.sharding import PartitionSpec as P

BF = jnp.bfloat16
F32 = jnp.float32


def gelu_slope(pre):
    cdf = 0.5 * (1.0 + jax.scipy.special.erf(pre * 0.7071067811865476))
    return cdf + pre * jnp.exp(-0.5 * pre * pre) * 0.3989422804014327


def swap(x):
    return lax.ppermute(x, "tok", [(0, 1), (1, 0)])


def mm(a, b, dims):
    return lax.dot_general(a, b, (dims, ((), ())), preferred_element_type=F32)


def after(x, *others):
    return lax.optimization_barrier((x,) + others)[0]


def send_partial(part, n):
    if n == 2:
        return part, lax.ppermute(part.astype(BF), "in", [(0, 1), (1, 0)])
    return None, lax.psum(part, "in")


def direct(x, n):
    return 1 < n <= 8 and x.shape[1] % (128 * n) == 0


def scatter_out(x, n):
    w = x.shape[1] // n
    me = lax.axis_index("out")
    total = lax.dynamic_slice_in_dim(x, me * w, w, 1)
    xb = x.astype(BF)
    for k in range(1, n):
        to = lax.rem(me + k, n)
        piece = lax.dynamic_slice_in_dim(xb, to * w, w, 1)
        got = lax.ppermute(piece, "out", [(i, (i + k) % n) for i in range(n)])
        total = total + got.astype(F32)
    return total.astype(BF), xb


def gather_out(mine, n):
    w = mine.shape[1]
    me = lax.axis_index("out")
    out = jnp.zeros((mine.shape[0], w * n), BF)
    out = lax.dynamic_update_slice_in_dim(out, mine, me * w, 1)
    for k in range(1, n):
        got = lax.ppermute(mine, "out", [(i, (i + k) % n) for i in range(n)])
        out = lax.dynamic_update_slice_in_dim(out, got, lax.rem(me - k + n, n) * w, 1)
    return out


def block_of(n, sizes):
    for b in sizes:
        if n % b == 0:
            return b
    return n


def dx_kernel(m_ref, o_ref, w_ref, sum_ref, acc_ref):
    i = pl.program_id(0)

    @pl.when(i == 0)
    def _():
        acc_ref[...] = jnp.zeros_like(acc_ref)

    g = jnp.concatenate([m_ref[...], o_ref[...]], axis=0)
    acc_ref[...] += lax.dot_general(
        w_ref[...], g, (((1,), (1,)), ((), ())), preferred_element_type=F32
    )

    @pl.when(i == pl.num_programs(0) - 1)
    def _():
        sum_ref[...] = acc_ref[...].T


def dx_partial(mine, other, weight, unit):
    rows = weight.shape[0]
    m, width = mine.shape
    g_block = pl.BlockSpec((m, unit), lambda i: (0, i))
    whole = pl.BlockSpec((2 * m, rows), lambda i: (0, 0))
    return pl.pallas_call(
        dx_kernel,
        grid=(width // unit,),
        in_specs=[
            g_block,
            g_block,
            pl.BlockSpec((rows, unit), lambda i: (0, i)),
        ],
        out_specs=whole,
        out_shape=jax.ShapeDtypeStruct((2 * m, rows), F32),
        scratch_shapes=[pltpu.VMEM((rows, 2 * m), F32)],
        cost_estimate=pl.CostEstimate(
            flops=4 * m * rows * width, bytes_accessed=2 * rows * width, transcendentals=0
        ),
        compiler_params=pltpu.CompilerParams(vmem_limit_bytes=48 * 2**20),
    )(mine, other, weight)


def score_kernel(parts, x_ref, *refs):
    g_refs, (w_ref, s_ref), o_ref = refs[:parts], refs[parts : parts + 2], refs[-1]
    rows = w_ref.shape[0]
    step = block_of(rows, (384, 256, 128))
    g = jnp.concatenate([ref[...] for ref in g_refs], axis=0)
    for r in range(0, rows, step):
        part = pl.ds(r, step)
        gw = jnp.dot(x_ref[part, :], g, preferred_element_type=F32)
        o_ref[part, :] = (
            s_ref[part, :].astype(F32) - w_ref[part, :].astype(F32) * gw
        ).astype(BF)


def score_part(x_t, gs, weight, score, first, count, w, earlier):
    rows, ff = weight.shape
    m, width = gs[0].shape[0], count * w
    block = pl.BlockSpec((rows, w), lambda i: (0, i + first))
    specs = [pl.BlockSpec(x_t.shape, lambda i: (0, 0))]
    specs += [pl.BlockSpec((m, w), lambda i: (0, i + first)) for _ in gs]
    specs += [block, block]
    args = [x_t, *gs, weight, score]
    alias = {}
    if earlier is not None:
        alias = {len(args): 0}
        specs.append(pl.BlockSpec(memory_space=pl.ANY))
        args.append(earlier)
    return pl.pallas_call(
        functools.partial(score_kernel, len(gs)),
        grid=(count,),
        in_specs=specs,
        out_specs=block,
        out_shape=jax.ShapeDtypeStruct((rows, ff), BF),
        input_output_aliases=alias,
        cost_estimate=pl.CostEstimate(
            flops=2 * x_t.shape[1] * rows * width,
            bytes_accessed=6 * rows * width,
            transcendentals=0,
        ),
        compiler_params=pltpu.CompilerParams(vmem_limit_bytes=40 * 2**20),
    )(*args)


def make(n_in, n_out):
    def on_device(inputs, grad_act, weight, score):
        rows, ff = weight.shape
        tokens = inputs.shape[0]
        t = lax.axis_index("tok")
        full = -(-tokens // 16) * 16
        pad = ((0, full - tokens), (0, 0))
        x_mine = lax.dynamic_slice_in_dim(inputs, t * rows, rows, 1)
        x_other = swap(lax.dynamic_slice_in_dim(inputs, (1 - t) * rows, rows, 1))
        chunks = 4 if ff % (4 * 256) == 0 else 1
        w = ff // chunks
        gm, go, sent = [], [], []
        unit = block_of(w, (512, 256, 128))
        for c in range(chunks):
            wc = weight[:, c * w : (c + 1) * w]
            send = mm(x_other, wc, ((1,), (0,))).astype(BF)
            part = mm(x_mine, wc, ((1,), (0,))) + swap(send).astype(F32)
            sent.append(send_partial(part, n_in))
        early = None
        for c, (own, got) in enumerate(sent):
            if 0 < c == chunks - 1:
                ga = [jnp.concatenate(x, axis=1) for x in (gm, go)]
                early = dx_partial(*ga, weight, unit)
                got = after(got, early)
            pre = got if own is None else own + got.astype(F32)
            g = (grad_act[:, c * w : (c + 1) * w].astype(F32) * gelu_slope(pre)).astype(BF)
            g = jnp.pad(g, pad)
            gm.append(g)
            go.append(swap(g))
        gs = [jnp.concatenate(gm, axis=1), jnp.concatenate(go, axis=1)]
        if early is None:
            total = dx_partial(*gs, weight, unit)
        else:
            last = jnp.concatenate([gm[-1], go[-1]], axis=0)
            total = early + mm(last, weight[:, ff - w :], ((1,), (1,)))
        mine, theirs = total[:tokens], total[full : full + tokens]
        got = swap(theirs.astype(BF)).astype(F32)
        left, right = jnp.where(t == 0, mine, got), jnp.where(t == 0, got, mine)
        term = jnp.concatenate([left, right], axis=1)
        if direct(term, n_out):
            piece, ready = scatter_out(term, n_out)
            waits = [ready, piece]
            grad_inputs = gather_out(piece, n_out)
        else:
            waits = [term, term]
            grad_inputs = lax.psum(term, "out").astype(BF)
        x_t = jnp.concatenate([jnp.pad(x_mine, pad), jnp.pad(x_other, pad)], axis=0).T
        blocks = ff // unit
        half = (blocks + 1) // 2
        new_score = None
        for wait, first, count in ((waits[0], 0, half), (waits[1], half, blocks - half)):
            if count:
                x_now = after(x_t, wait)
                new_score = score_part(
                    x_now, gs, weight, score, first, count, unit, new_score
                )
        return grad_inputs, new_score

    return on_device


def solution(mesh):
    placed = (
        P(("group", "tok"), "in"),
        P(("group", "tok"), "out"),
        P(("in", "tok"), "out"),
        P(("in", "tok"), "out"),
    )
    return jax.shard_map(
        make(mesh.shape["in"], mesh.shape["out"]),
        mesh=mesh,
        in_specs=placed,
        out_specs=(P(("group", "tok"), "in"), P(("group", "in", "tok"), "out")),
        check_vma=False,
    )
```
